1024 devices in a mesh: dp: 8 (over x, core), expert: 32 (over z), head: 4 (over y).
Axes of the slice: x: 4, y: 4, z: 32, core: 2. Of those that a mesh axis runs over, the one named last changes fastest.
Arguments:
- latent: bfloat16 [10240, 1024], P(('dp', 'expert')), may hold values from -6 to 6
- cotangent: bfloat16 [10240, 1024], P(('dp', 'expert')), may hold values from -6 to 6
- routes: int32 [10240, 8], P(('dp', 'expert')), may hold values from 0 to 63, all different within a row; in each aligned block of 40 rows (0 to 39, 40 to 79, ...) at most 6 rows name the same one
- gate_values: float32 [10240, 8], P(('dp', 'expert')), may hold values from 0.05 to 0.5
- weight_in: bfloat16 [64, 2048, 1024], P('expert', 'head'), may hold values from -0.1875 to 0.1875
- weight_out: bfloat16 [64, 2048, 1024], P('expert', 'head'), may hold values from -0.125 to 0.125
Outputs:
- moe_out: bfloat16 [10240, 1024], P(('dp', 'expert'))
- latent_grad: bfloat16 [10240, 1024], P(('dp', 'expert'))
- weight_in_grad: bfloat16 [64, 2048, 1024], P('expert', 'head', 'dp')
- weight_out_grad: bfloat16 [64, 2048, 1024], P('expert', 'head', 'dp')
The draws below stay inside these ranges and needn't reach their ends.
Inputs may be any that keep to these rules, and one draw needn't show every extreme that they name: `routes`: each row names 8 different experts. Among the rows of one device (40 rows in an aligned block), no expert is named by more than 6 rows, a bound that some block reaches.
All inputs are finite; a program needn't handle non-finite values.
Results may differ from the reference program's by a relative error of at most 0.017.
Values may be sent and summed in bfloat16 or wider, within the bound.
A program may use at most 64 MiB of HBM per device.

```python
import math
import jax
import jax.numpy as jnp
import numpy as np
from jax import lax

LATENT = 1024
HIDDEN_SIZE = 2048
TOPK = 8
TOK_DEV = 40
EXPERTS = 64
CAP = 6
TOKENS = 10240
N_DP = 8
N_EXPERT = 32
N_HEAD = 4


def levels(stream_key, extent, shards, least, largest):
    def one(position, blocks):
        steps = jax.random.uniform(jax.random.fold_in(jax.random.fold_in(stream_key, 6), position), (blocks,), jnp.float32, least / len(shards), largest / len(shards))
        return jnp.repeat(jnp.exp(steps), extent[position] // blocks).reshape((-1,) + (1,) * (len(extent) - position - 1))

    level = one(*shards[0])
    for cut in shards[1:]:
        level = level * one(*cut)
    return level


def assign_block(stream_key, own, number, rows, amount, top, most, slope):
    ranking = jax.random.permutation(stream_key, amount)
    heavy_load, ordinary = portions_of(amount, rows * top, most, slope, True), portions_of(amount, rows * top, most, slope, False)
    places = jnp.arange(amount)

    def named(lengths, rotation):
        used = int((lengths > 0).sum())
        fixed = max(1, used // 4)
        passed = fixed + (places - fixed + rotation * (used - fixed)) % max(1, amount - fixed)
        return jnp.zeros((amount,), jnp.int32).at[ranking[jnp.where(places < fixed, places, passed)]].set(jnp.asarray(lengths, jnp.int32))

    lengths = jnp.where(number % 4 == 0, named(heavy_load, number // 4), named(ordinary, number - number // 4 - 1))
    mixed = jax.random.permutation(jax.random.fold_in(own, 3), amount)
    giver, sink = mixed[0:amount // 2 * 2:2], mixed[1:amount // 2 * 2:2]
    room = jnp.minimum(lengths[giver] - 1, most - lengths[sink]) // 2
    room = jnp.where((giver == ranking[0]) | (sink == ranking[0]) | (lengths[sink] == 0), 0, jnp.maximum(room, 0))
    passed = jax.random.randint(jax.random.fold_in(own, 4), (amount // 2,), 0, 1 << 20) % (room + 1)
    lengths = lengths.at[giver].add(-passed).at[sink].add(passed)
    labels = jnp.searchsorted(jnp.cumsum(lengths), jnp.arange(rows * top), side="right").astype(jnp.int32)
    listing = labels.reshape(top, rows).T
    listing = listing[jax.random.permutation(jax.random.fold_in(own, 1), rows)]
    rotation = jax.random.randint(jax.random.fold_in(own, 2), (rows, 1), 0, top)
    return jnp.take_along_axis(listing, (jnp.arange(top)[None, :] + rotation) % top, axis=1)


def portions_of(number_of, total, most, skew, full):
    loads = [(1 << 20) // math.isqrt(standing ** skew) + 1 for standing in range(1, number_of + 1)]
    largest = most if full else min(most, max(-(-total // number_of), total * loads[0] // sum(loads)))
    least = 1 if total - largest >= number_of - 1 else 0
    counts, spare = [largest] + [least] * (number_of - 1), total - largest - least * (number_of - 1)
    while spare > 0:
        free = [i for i in range(1, number_of) if counts[i] < largest] or [i for i in range(1, number_of) if counts[i] < most]
        pool, left = sum([loads[i] for i in free]), spare
        for i in free:
            addition = min(most - counts[i], max(1, left * loads[i] // pool), spare)
            counts[i] = counts[i] + addition
            spare = spare - addition
    return np.array(counts)


def scatter_about(rng, dims, scale, reach, split=(), kind=jnp.bfloat16):
    entries = jax.random.normal(rng, dims, jnp.float32) * scale
    if len(split) > 0:
        entries = levels(rng, dims, split, -0.22, 0.18) * entries
    return jnp.clip(entries, min=-reach, max=reach).astype(kind)


def setup_inputs(seed: int = 0) -> dict:
    keys = jax.random.split(jax.random.key(seed), 7)
    latent = scatter_about(keys[0], (TOKENS, LATENT), 1.0, 6.0, ((0, 256),))
    cotangent = scatter_about(keys[1], (TOKENS, LATENT), 1.0, 6.0, ((0, 256),))
    routes_keys = jax.random.split(jax.random.fold_in(keys[2], 1), TOKENS // TOK_DEV)
    routes_turns = jax.random.permutation(jax.random.fold_in(keys[2], 3), TOKENS // TOK_DEV)
    routes = jax.vmap(lambda own, number: assign_block(jax.random.fold_in(keys[2], 2), own, number, TOK_DEV, EXPERTS, TOPK, CAP, 2))(routes_keys, routes_turns).reshape((TOKENS, TOPK))
    gate_values = jnp.clip(jnp.exp(math.log(0.5) - 2.3025851 * jax.random.uniform(keys[3], (TOKENS, TOPK), jnp.float32) ** levels(keys[3], (TOKENS, TOPK), ((0, 256),), -0.2, 0.2)), 0.05, 0.5)
    weight_in = scatter_about(keys[4], (EXPERTS, HIDDEN_SIZE, LATENT), LATENT ** -0.5, 0.1875, ((0, 32), (1, 4)))
    weight_out = scatter_about(keys[5], (EXPERTS, HIDDEN_SIZE, LATENT), HIDDEN_SIZE ** -0.5, 0.125, ((0, 32), (1, 4)))
    return {"latent": latent, "cotangent": cotangent, "routes": routes, "gate_values": gate_values, "weight_in": weight_in, "weight_out": weight_out}


def rounded(values):
    return lax.optimization_barrier(values.astype(jnp.bfloat16)).astype(jnp.float32)


def block_ranks(block_routes):
    flat_routes = block_routes.reshape(-1)
    onehot = (flat_routes[:, None] == jnp.arange(EXPERTS, dtype=jnp.int32)[None, :]).astype(jnp.int32)
    before = jnp.cumsum(onehot, axis=0) - onehot
    return jnp.sum(before * onehot, axis=1).astype(jnp.int32)


def reference(latent, cotangent, routes, gate_values, weight_in, weight_out):
    sources = N_DP * N_EXPERT
    slot_depth = sources * CAP
    block_width = HIDDEN_SIZE // N_HEAD
    route_rank = jax.vmap(block_ranks)(routes.reshape(sources, TOK_DEV, TOPK)).reshape(-1)
    anchor = jnp.arange(TOKENS * TOPK, dtype=jnp.int32) // (TOK_DEV * TOPK)
    route_slot = (anchor * CAP + route_rank).astype(jnp.int32)
    expert = routes.reshape(-1).astype(jnp.int32)
    token_index = jnp.arange(TOKENS * TOPK, dtype=jnp.int32) // TOPK
    scaled = (gate_values.reshape(-1)[:, None] * cotangent[token_index].astype(jnp.float32)).astype(jnp.bfloat16)
    rows_in = jnp.zeros((EXPERTS, slot_depth, LATENT), jnp.bfloat16).at[expert, route_slot].set(latent[token_index])
    grads_in = jnp.zeros((EXPERTS, slot_depth, LATENT), jnp.bfloat16).at[expert, route_slot].set(scaled)

    def one_expert(operands):
        rows_local, grads_local, in_matrix, out_matrix = operands
        rows_wide = rows_local.astype(jnp.float32)
        grads_wide = grads_local.astype(jnp.float32)
        in_wide = in_matrix.astype(jnp.float32)
        out_wide = out_matrix.astype(jnp.float32)
        pre_act = jnp.dot(rows_wide, in_wide.T, preferred_element_type=jnp.float32)
        positive = jnp.maximum(pre_act, 0.0)
        hidden_act = rounded(positive * positive)
        out_part = rounded(jnp.einsum("rhk,hkl->rhl", hidden_act.reshape(slot_depth, N_HEAD, block_width),
                                      out_wide.reshape(N_HEAD, block_width, LATENT)))
        out_sum = jnp.sum(out_part, axis=1)
        grad_act = jnp.dot(grads_wide, out_wide.T, preferred_element_type=jnp.float32)
        grad_pre = rounded(grad_act * 2.0 * positive)
        back_part = rounded(jnp.einsum("rhk,hkl->rhl", grad_pre.reshape(slot_depth, N_HEAD, block_width),
                                       in_wide.reshape(N_HEAD, block_width, LATENT)))
        back_sum = jnp.sum(back_part, axis=1)
        group_rows = slot_depth // N_DP
        act_groups = hidden_act.reshape(N_DP, group_rows, HIDDEN_SIZE)
        pre_groups = grad_pre.reshape(N_DP, group_rows, HIDDEN_SIZE)
        grads_groups = grads_wide.reshape(N_DP, group_rows, LATENT)
        rows_groups = rows_wide.reshape(N_DP, group_rows, LATENT)
        out_grad = jnp.sum(rounded(jnp.einsum("drh,drl->dhl", act_groups, grads_groups)), axis=0).astype(jnp.bfloat16)
        in_grad = jnp.sum(rounded(jnp.einsum("drh,drl->dhl", pre_groups, rows_groups)), axis=0).astype(jnp.bfloat16)
        return out_sum, back_sum, in_grad, out_grad

    out_sum, back_sum, weight_in_grad, weight_out_grad = lax.map(one_expert, (rows_in, grads_in, weight_in, weight_out))
    picked_out = out_sum[expert, route_slot].reshape(TOKENS, TOPK, LATENT)
    picked_back = back_sum[expert, route_slot].reshape(TOKENS, TOPK, LATENT)
    moe_out = jnp.sum(gate_values[:, :, None] * picked_out, axis=1).astype(jnp.bfloat16)
    latent_grad = jnp.sum(picked_back, axis=1).astype(jnp.bfloat16)
    return moe_out, latent_grad, weight_in_grad, weight_out_grad
```

```python
import jax
import jax.numpy as jnp
from jax import lax
from jax.sharding import PartitionSpec as P

CAPACITY = 6


def on_device(latent, cotangent, routes, gate_values, weight_in, weight_out):
    token_count, latent_width = latent.shape
    route_count = routes.shape[1]
    owners = lax.axis_size("expert")
    heads = lax.axis_size("head")
    local = weight_in.shape[0]
    quarter = latent_width // heads
    me = lax.axis_index("expert")
    head = lax.axis_index("head")
    slots = local * CAPACITY
    f32, bf16 = jnp.float32, jnp.bfloat16

    own = lax.dynamic_slice(
        jnp.concatenate([latent, cotangent], 0), (0, head * quarter), (2 * token_count, quarter)
    )
    meta = jnp.concatenate([routes.astype(f32), gate_values], axis=1)
    meta = lax.all_gather(meta, "expert", axis=0)
    data = lax.all_gather(own, "expert", axis=0)

    expert = (me * local + jnp.arange(local)).astype(f32)
    hit = meta[:, :, None, :route_count] == expert[None, None, :, None]
    chosen = jnp.any(hit, axis=3)
    gates = jnp.sum(jnp.where(hit, meta[:, :, None, route_count:], 0.0), axis=3)
    count = chosen.astype(jnp.int32)
    rank = jnp.cumsum(count, axis=1) - count
    place = (rank[..., None] == jnp.arange(CAPACITY)) & chosen[..., None]
    gate_slot = jnp.sum(jnp.where(place, gates[..., None], 0.0), axis=1)
    gate_slot = gate_slot.reshape(owners, slots, 1)
    place = place.astype(bf16).reshape(owners, token_count, slots)

    rows = jnp.einsum("stc,stl->scl", place, data[:, :token_count], preferred_element_type=f32)
    grads = jnp.einsum("stc,stl->scl", place, data[:, token_count:], preferred_element_type=f32)
    both = jnp.stack([rows.astype(bf16), (grads * gate_slot).astype(bf16)])
    both = lax.all_gather(both, "head", axis=3, tiled=True)
    both = both.reshape(2, owners, local, CAPACITY, latent_width)
    got = both.transpose(0, 2, 1, 3, 4).reshape(2, local, owners * CAPACITY, latent_width)
    got_rows, got_grads = got[0], got[1]

    pre_act = jnp.einsum("ecl,ehl->ech", got_rows, weight_in, preferred_element_type=f32)
    positive = jnp.maximum(pre_act, 0.0)
    hidden_act = (positive * positive).astype(bf16)
    out_part = jnp.einsum("ech,ehl->ecl", hidden_act, weight_out, preferred_element_type=f32)
    grad_act = jnp.einsum("ecl,ehl->ech", got_grads, weight_out, preferred_element_type=f32)
    grad_pre = (grad_act * 2.0 * positive).astype(bf16)
    back_part = jnp.einsum("ech,ehl->ecl", grad_pre, weight_in, preferred_element_type=f32)
    parts = jnp.stack([out_part.astype(bf16), back_part.astype(bf16)])
    share = lax.psum_scatter(parts, "head", scatter_dimension=3, tiled=True)
    in_partial = jnp.einsum("ech,ecl->ehl", grad_pre, got_rows, preferred_element_type=f32)
    out_partial = jnp.einsum("ech,ecl->ehl", hidden_act, got_grads, preferred_element_type=f32)
    partial = jnp.stack([in_partial.astype(bf16), out_partial.astype(bf16)])
    summed = lax.psum_scatter(partial, "dp", scatter_dimension=3, tiled=True)

    share = share.reshape(2, local, owners, CAPACITY, quarter).transpose(0, 2, 1, 3, 4)
    share = share.reshape(2, owners, slots, quarter)
    scaled = (share[0].astype(f32) * gate_slot).astype(bf16)
    out_tok = jnp.einsum("stc,scl->stl", place, scaled, preferred_element_type=f32)
    back_tok = jnp.einsum("stc,scl->stl", place, share[1], preferred_element_type=f32)
    tokens = jnp.stack([out_tok.astype(bf16), back_tok.astype(bf16)], axis=1)
    mine = lax.psum_scatter(tokens, "expert", scatter_dimension=0)
    full = lax.all_gather(mine, "head", axis=2, tiled=True)
    return full[0], full[1], summed[0], summed[1]


def solution(mesh):
    in_specs = (
        P(("dp", "expert"), None),
        P(("dp", "expert"), None),
        P(("dp", "expert"), None),
        P(("dp", "expert"), None),
        P("expert", "head", None),
        P("expert", "head", None),
    )
    out_specs = (
        P(("dp", "expert"), None),
        P(("dp", "expert"), None),
        P("expert", "head", "dp"),
        P("expert", "head", "dp"),
    )
    return jax.shard_map(
        on_device, mesh=mesh, in_specs=in_specs, out_specs=out_specs, check_vma=False
    )
```

```python
import functools

import jax
import jax.numpy as jnp
from jax import lax
from jax.experimental import pallas as pl
from jax.experimental.pallas import tpu as pltpu
from jax.sharding import PartitionSpec as P

CAPACITY = 6
GROUP = 8
MESH = pl.DeviceIdType.MESH
f32, bf16 = jnp.float32, jnp.bfloat16


def nt_dot(a, b):
    return lax.dot_general(a, b, (((1,), (1,)), ((), ())), preferred_element_type=f32)


def nn_dot(a, b):
    return lax.dot_general(a, b, (((1,), (0,)), ((), ())), preferred_element_type=f32)


def tn_dot(a, b):
    return lax.dot_general(a, b, (((0,), (0,)), ((), ())), preferred_element_type=f32)


def kernel(
    dims, blk_ref, win_hbm, wout_hbm, tok_ref, wgrad_ref,
    ring, picks, gates, xrows, win, wout, acts, yown, yland, contrib, from_left, from_right,
    parts, pair, cross,
    w_sem, zs, zr, ys, yr, os_, or_, rs, rr, ps, pr, cs, cr, ts, tr,
):
    owners, heads, xs, tokens, local = dims
    half = owners // 2
    chunks = owners // GROUP
    rows = GROUP * CAPACITY
    both = 2 * tokens
    width = ring.shape[2]
    hidden = win.shape[1]
    pieces = hidden // 256

    me = lax.axis_index("expert")
    head = lax.axis_index("head")
    dp = lax.axis_index("dp")
    px, core = dp // 2, dp % 2
    right, left = lax.rem(me + 1, owners), lax.rem(me + owners - 1, owners)
    to_right, to_left = {"expert": right}, {"expert": left}
    head_at = [lax.rem(head + d, heads) for d in range(heads)]
    x_at = [lax.rem(px + d, xs) for d in range(xs)]
    sibling = {"dp": px * 2 + 1 - core}

    def remote(src, dst, send, recv, device):
        return pltpu.make_async_remote_copy(
            src_ref=src, dst_ref=dst, send_sem=send, recv_sem=recv,
            device_id=device, device_id_type=MESH,
        )

    load_in = pltpu.make_async_copy(win_hbm, win, w_sem.at[0])
    load_out = pltpu.make_async_copy(wout_hbm, wout, w_sem.at[1])
    load_in.start()
    load_out.start()
    ring[0] = blk_ref[...]

    barrier = pltpu.get_barrier_semaphore()
    partners = [to_right, to_left, sibling]
    partners += [{"head": head_at[d]} for d in range(1, heads)]
    partners += [{"dp": x_at[d] * 2 + core} for d in range(1, xs)]
    for device in partners:
        pl.semaphore_signal(barrier, inc=1, device_id=device, device_id_type=MESH)
    pl.semaphore_wait(barrier, len(partners))

    def slot_right(i):
        return jnp.maximum(2 * i - 1, 0)

    def ring_right(i):
        return remote(
            ring.at[slot_right(i - 1)], ring.at[slot_right(i)], zs.at[0, i], zr.at[0, i], to_right
        )

    def ring_left(i):
        return remote(ring.at[2 * (i - 1)], ring.at[2 * i], zs.at[1, i], zr.at[1, i], to_left)

    def spread(d, c):
        return remote(
            xrows.at[head, c], xrows.at[head, c], ys.at[d - 1, c], yr.at[d - 1, c],
            {"head": head_at[d]},
        )

    ring_right(1).start()
    ring_left(1).start()

    lane = lax.broadcasted_iota(jnp.int32, (128, 128), 1)
    depth = lax.broadcasted_iota(jnp.int32, (128, 128), 0)
    earlier = (depth < lane) & ((depth < tokens) == (lane < tokens))
    earlier = jnp.where(earlier, 1.0, 0.0).astype(bf16)
    row_id = lax.broadcasted_iota(jnp.int32, (rows, 128), 0).astype(f32)
    group_row = lax.broadcasted_iota(jnp.int32, (GROUP, 128), 0).astype(f32) * CAPACITY
    group_lane = lax.broadcasted_iota(jnp.int32, (GROUP, 128), 1)

    def select(c):
        meta = ring[pl.ds(c * GROUP, GROUP), both:both + 16, :].astype(f32)
        routes = meta[:, :8, :128]
        gate = meta[:, 8:, :128] + meta[:, :8, 128:] + meta[:, 8:, 128:]
        codes, weights = [], []
        for e in range(local):
            hit = routes == (me * local + e).astype(f32)
            chosen = jnp.max(jnp.where(hit, 1.0, 0.0), axis=1)
            weights.append(jnp.sum(jnp.where(hit, gate, 0.0), axis=1))
            rank = nn_dot(chosen.astype(bf16), earlier)
            codes.append(jnp.where(chosen > 0.5, rank + group_row, -1.0))
        by_kind = [jnp.where(group_lane < tokens, code, -1.0) for code in codes]
        by_kind += [jnp.where(group_lane >= tokens, code, -1.0) for code in codes]
        total = jnp.zeros((2 * local * rows, width), f32)
        scale = [jnp.zeros((rows, 128), f32) for _ in range(local)]
        for q in range(GROUP):
            match = [row_id == code[q:q + 1, :] for code in by_kind]
            pick = jnp.concatenate([jnp.where(m, 1.0, 0.0) for m in match], axis=0).astype(bf16)
            picks[c * GROUP + q] = pick
            block = ring[c * GROUP + q]
            total = total + nn_dot(pick[:, :both + 16], block)
            for e in range(local):
                scale[e] = scale[e] + jnp.where(match[local + e], weights[e][q:q + 1, :], 0.0)
        scale = jnp.sum(jnp.concatenate(scale, axis=0), axis=1, keepdims=True)
        gates[c] = jnp.broadcast_to(scale, (local * rows, 128))
        xrows[head, c, 0] = total[: local * rows].astype(bf16).reshape(local, rows, width)
        xrows[head, c, 1] = (total[local * rows:] * scale).astype(bf16).reshape(local, rows, width)

    def gather_group(c, carry):
        for k in range(4):
            i = c * 4 + 1 + k
            ring_right(i).wait_recv()

            @pl.when(i < half)
            def _():
                ring_right(i + 1).start()
                ring_left(i).wait_recv()

            @pl.when(i < half - 1)
            def _():
                ring_left(i + 1).start()

        select(c)
        for d in range(1, heads):
            spread(d, c).start()
        return carry

    lax.fori_loop(0, chunks, gather_group, 0)
    load_in.wait()
    load_out.wait()

    def spread_wait(c, carry):
        for d in range(1, heads):
            spread(d, c).wait()
        return carry

    lax.fori_loop(0, chunks, spread_wait, 0)

    def taken(kind, e, h):
        return xrows[h, :, kind, e].reshape(chunks * rows, width)

    def expert(e, carry):
        got = [jnp.concatenate([taken(k, e, h) for h in range(heads)], axis=1) for k in range(2)]
        for p in range(pieces):
            part = pl.ds(p * 256, 256)
            positive = jnp.maximum(nt_dot(got[0], win[e, part, :]), 0.0)
            acts[0, e, p] = (positive * positive).astype(bf16)
            grad = nt_dot(got[1], wout[e, part, :])
            acts[1, e, p] = (grad * 2.0 * positive).astype(bf16)
        for k, weight in ((0, wout), (1, win)):
            act = jnp.concatenate([acts[k, e, p] for p in range(pieces)], axis=1)
            for h in range(heads):
                out = nn_dot(act, weight[e, :, h * width:(h + 1) * width])
                yown[h, :, k, e] = out.astype(bf16).reshape(chunks, rows, width)
        return carry

    lax.fori_loop(0, local, expert, 0)

    def share(d, c):
        return remote(
            yown.at[head_at[d], c], yland.at[d - 1, c], os_.at[d - 1, c], or_.at[d - 1, c],
            {"head": head_at[d]},
        )

    def share_start(k, carry):
        for d in range(1, heads):
            share(d, chunks - 1 - k).start()
        return carry

    lax.fori_loop(0, chunks, share_start, 0)

    def weight_grads(e, carry):
        for p in range(pieces):
            for h in range(heads):
                for w in range(2):
                    piece = tn_dot(acts[1 - w, e, p], taken(w, e, h)).astype(bf16)
                    for s in range(width // 128):
                        dest = h * (width // 128) + s
                        parts[dest % 2, dest // 2, w, e, p * 256:(p + 1) * 256, :] = (
                            piece[:, s * 128:(s + 1) * 128]
                        )
        return carry

    lax.fori_loop(0, local, weight_grads, 0)
    pair_copy = remote(parts.at[1 - core], pair, ps.at[0], pr.at[0], sibling)
    pair_copy.start()

    def combine(c):
        for d in range(1, heads):
            share(d, c).wait_recv()
        total = yown[head, c].astype(f32)
        for d in range(1, heads):
            total = total + yland[d - 1, c].astype(f32)
        out = total[0].reshape(local * rows, width) * gates[c][:, :1]
        back = total[1].reshape(local * rows, width)
        total = jnp.concatenate([out, back], axis=0).astype(bf16)
        for q in range(GROUP):
            contrib[c * GROUP + q] = tn_dot(picks[c * GROUP + q], total)[:both].astype(bf16)

    def target_right(j):
        return 2 * (half - j) - jnp.where(j == 0, 1, 0)

    def target_left(j):
        return 2 * (half - 1 - j) - 1

    def sum_right(j):
        return remote(
            contrib.at[target_right(j)], from_left.at[j], rs.at[0, j], rr.at[0, j], to_right
        )

    def sum_left(j):
        return remote(
            contrib.at[target_left(j)], from_right.at[j], rs.at[1, j], rr.at[1, j], to_left
        )

    def cross_copy(d):
        return remote(
            parts.at[core, x_at[d]], cross.at[d - 1], cs.at[d - 1], cr.at[d - 1],
            {"dp": x_at[d] * 2 + core},
        )

    combine(chunks - 1)

    def add(a, b):
        return (a.astype(f32) + b.astype(f32)).astype(bf16)

    def sum_step(j, carry):
        @pl.when(j > 0)
        def _():
            sum_right(j - 1).wait_recv()
            to = target_right(j)
            contrib[to] = add(contrib[to], from_left[j - 1])

        sum_right(j).start()

        @pl.when((j > 0) & (j < half - 1))
        def _():
            sum_left(j - 1).wait_recv()
            to = target_left(j)
            contrib[to] = add(contrib[to], from_right[j - 1])

        @pl.when(j < half - 1)
        def _():
            sum_left(j).start()

        @pl.when((lax.rem(j, 4) == 2) & (j < half - 4))
        def _():
            combine(chunks - 2 - j // 4)

        @pl.when(j == 1)
        def _():
            pair_copy.wait()

            def merge(k, inner):
                x, w, e = k // (2 * local), (k // local) % 2, k % local
                parts[core, x, w, e] = add(parts[core, x, w, e], pair[x, w, e])
                return inner

            lax.fori_loop(0, xs * 2 * local, merge, 0)
            for d in range(1, xs):
                cross_copy(d).start()

        return carry

    lax.fori_loop(0, half, sum_step, 0)
    sum_right(half - 1).wait_recv()
    sum_left(half - 2).wait_recv()
    mine = contrib[0].astype(f32) + from_left[half - 1].astype(f32)
    mine = (mine + from_right[half - 2].astype(f32)).astype(bf16)
    columns = pl.ds(pl.multiple_of(head * width, width), width)
    tok_ref[:, columns] = mine

    def tell(d):
        return remote(
            tok_ref.at[:, columns], tok_ref.at[:, columns], ts.at[d - 1], tr.at[d - 1],
            {"head": head_at[d]},
        )

    for d in range(1, heads):
        tell(d).start()
    for d in range(1, xs):
        cross_copy(d).wait()

    def finish(k, carry):
        w, e = k // local, k % local
        total = parts[core, px, w, e].astype(f32)
        for d in range(1, xs):
            total = total + cross[d - 1, w, e].astype(f32)
        wgrad_ref[w, e] = total.astype(bf16)
        return carry

    lax.fori_loop(0, 2 * local, finish, 0)

    def drain_ring(i, carry):
        ring_right(i).wait_send()
        sum_right(i - 1).wait_send()

        @pl.when(i < half)
        def _():
            ring_left(i).wait_send()
            sum_left(i - 1).wait_send()

        return carry

    lax.fori_loop(1, half + 1, drain_ring, 0)

    def drain_share(c, carry):
        for d in range(1, heads):
            share(d, c).wait_send()
        return carry

    lax.fori_loop(0, chunks, drain_share, 0)
    for d in range(1, heads):
        tell(d).wait()


def on_device(latent, cotangent, routes, gate_values, weight_in, weight_out):
    tokens, latent_width = latent.shape
    owners = lax.axis_size("expert")
    heads = lax.axis_size("head")
    xs = lax.axis_size("dp") // 2
    local, hidden, _ = weight_in.shape
    width = latent_width // heads
    head = lax.axis_index("head")
    both = 2 * tokens
    half = owners // 2
    chunks = owners // GROUP
    rows = GROUP * CAPACITY

    data = jnp.concatenate([latent, cotangent], 0)
    data = lax.dynamic_slice(data, (0, head * width), (both, width))
    named = routes.T.astype(f32)
    gate = gate_values.T
    high = lax.reduce_precision(gate, 8, 7)
    middle = lax.reduce_precision(gate - high, 8, 7)
    low = lax.reduce_precision(gate - high - middle, 8, 7)

    def on_grads(piece):
        return jnp.pad(piece, ((0, 0), (tokens, 128 - both)))

    named = jnp.pad(
        jnp.concatenate([named, named], 1), ((0, 0), (0, 128 - both)), constant_values=-1.0
    )
    meta = jnp.concatenate(
        [
            jnp.concatenate([named, on_grads(middle)], 1),
            jnp.concatenate([on_grads(high), on_grads(low)], 1),
        ],
        0,
    )
    block = jnp.concatenate([data, meta.astype(bf16)], 0)

    dma = pltpu.SemaphoreType.DMA
    vmem = pltpu.VMEM
    tokens_out, grads_out = pl.pallas_call(
        functools.partial(kernel, (owners, heads, xs, tokens, local)),
        out_shape=(
            jax.ShapeDtypeStruct((both, latent_width), bf16),
            jax.ShapeDtypeStruct((2, local, hidden, 128), bf16),
        ),
        in_specs=[
            pl.BlockSpec(memory_space=pltpu.VMEM),
            pl.BlockSpec(memory_space=pl.ANY),
            pl.BlockSpec(memory_space=pl.ANY),
        ],
        out_specs=(
            pl.BlockSpec(memory_space=pltpu.VMEM),
            pl.BlockSpec(memory_space=pltpu.VMEM),
        ),
        scratch_shapes=[
            vmem((owners, both + 16, width), bf16),
            vmem((owners, 2 * local * rows, 128), bf16),
            vmem((chunks, local * rows, 128), f32),
            vmem((heads, chunks, 2, local, rows, width), bf16),
            vmem((local, hidden, latent_width), bf16),
            vmem((local, hidden, latent_width), bf16),
            vmem((2, local, hidden // 256, chunks * rows, 256), bf16),
            vmem((heads, chunks, 2, local, rows, width), bf16),
            vmem((heads - 1, chunks, 2, local, rows, width), bf16),
            vmem((owners, both, width), bf16),
            vmem((half, both, width), bf16),
            vmem((half - 1, both, width), bf16),
            vmem((2, xs, 2, local, hidden, 128), bf16),
            vmem((xs, 2, local, hidden, 128), bf16),
            vmem((xs - 1, 2, local, hidden, 128), bf16),
            dma((2,)),
            dma((2, half + 1)),
            dma((2, half + 1)),
            dma((heads - 1, chunks)),
            dma((heads - 1, chunks)),
            dma((heads - 1, chunks)),
            dma((heads - 1, chunks)),
            dma((2, half)),
            dma((2, half)),
            dma((1,)),
            dma((1,)),
            dma((xs - 1,)),
            dma((xs - 1,)),
            dma((heads - 1,)),
            dma((heads - 1,)),
        ],
        compiler_params=pltpu.CompilerParams(
            collective_id=0, has_side_effects=True, vmem_limit_bytes=48 * 1024 * 1024
        ),
        name="experts",
    )(block, weight_in, weight_out)
    return tokens_out[:tokens], tokens_out[tokens:], grads_out[0], grads_out[1]


def solution(mesh):
    in_specs = (
        P(("dp", "expert"), None),
        P(("dp", "expert"), None),
        P(("dp", "expert"), None),
        P(("dp", "expert"), None),
        P("expert", "head", None),
        P("expert", "head", None),
    )
    out_specs = (
        P(("dp", "expert"), None),
        P(("dp", "expert"), None),
        P("expert", "head", "dp"),
        P("expert", "head", "dp"),
    )
    return jax.shard_map(
        on_device, mesh=mesh, in_specs=in_specs, out_specs=out_specs, check_vma=False
    )
```

```python
import functools

import jax
import jax.numpy as jnp
from jax import lax
from jax.experimental import pallas as pl
from jax.experimental.pallas import tpu as pltpu
from jax.sharding import PartitionSpec as P

CAPACITY = 6
GROUP = 8
MESH = pl.DeviceIdType.MESH
f32, bf16 = jnp.float32, jnp.bfloat16


def nt_dot(a, b):
    return lax.dot_general(a, b, (((1,), (1,)), ((), ())), preferred_element_type=f32)


def nn_dot(a, b):
    return lax.dot_general(a, b, (((1,), (0,)), ((), ())), preferred_element_type=f32)


def tn_dot(a, b):
    return lax.dot_general(a, b, (((0,), (0,)), ((), ())), preferred_element_type=f32)


def kernel(
    dims, blk_ref, win_hbm, wout_hbm, tok_ref, wgrad_ref,
    ring, picks, gates, xrows, win, wout, acts, yown, yland, contrib, landed,
    parts, pair, cross,
    w_sem, zs, zr, ys, yr, os_, or_, rs, rr, ps, pr, cs, cr, ts, tr,
):
    owners, heads, xs, tokens, local = dims
    half = owners // 2
    hops = half // 2
    chunks = owners // GROUP
    rows = GROUP * CAPACITY
    both = 2 * tokens
    width = ring.shape[2]
    hidden = win.shape[1]
    pieces = hidden // 256

    me = lax.axis_index("expert")
    head = lax.axis_index("head")
    dp = lax.axis_index("dp")
    px, core = dp // 2, dp % 2
    ahead = [{"expert": lax.rem(me + d, owners)} for d in (1, 2)]
    behind = [{"expert": lax.rem(me + owners - d, owners)} for d in (1, 2)]
    head_at = [lax.rem(head + d, heads) for d in range(heads)]
    x_at = [lax.rem(px + d, xs) for d in range(xs)]
    sibling = {"dp": px * 2 + 1 - core}

    def remote(src, dst, send, recv, device):
        return pltpu.make_async_remote_copy(
            src_ref=src, dst_ref=dst, send_sem=send, recv_sem=recv,
            device_id=device, device_id_type=MESH,
        )

    load_in = pltpu.make_async_copy(win_hbm, win, w_sem.at[0])
    load_out = pltpu.make_async_copy(wout_hbm, wout, w_sem.at[1])
    load_in.start()
    load_out.start()
    ring[0] = blk_ref[...]

    barrier = pltpu.get_barrier_semaphore()
    partners = ahead + behind + [sibling]
    partners += [{"head": head_at[d]} for d in range(1, heads)]
    partners += [{"dp": x_at[d] * 2 + core} for d in range(1, xs)]
    for device in partners:
        pl.semaphore_signal(barrier, inc=1, device_id=device, device_id_type=MESH)
    pl.semaphore_wait(barrier, len(partners))

    def slot_ahead(d):
        return jnp.maximum(2 * d - 1, 0)

    def piece_of(s, total):
        return pl.ds(0, 48) if s == 0 else pl.ds(48, total - 48)

    def go_ahead(k, side, s):
        to, part = 2 * k - side, piece_of(s, both + 16)
        return remote(
            ring.at[slot_ahead(2 * k - 2), part], ring.at[slot_ahead(to), part],
            zs.at[0, to, s], zr.at[0, to, s], ahead[1 - side],
        )

    def go_behind(k, side, s):
        to, part = 2 * k - side, piece_of(s, both + 16)
        return remote(
            ring.at[2 * (2 * k - 2), part], ring.at[2 * to, part],
            zs.at[1, to, s], zr.at[1, to, s], behind[1 - side],
        )

    def spread(d, c):
        return remote(
            xrows.at[head, c], xrows.at[head, c], ys.at[d - 1, c], yr.at[d - 1, c],
            {"head": head_at[d]},
        )

    for side in (0, 1):
        for s in (0, 1):
            go_ahead(1, side, s).start()
            go_behind(1, side, s).start()

    lane = lax.broadcasted_iota(jnp.int32, (128, 128), 1)
    depth = lax.broadcasted_iota(jnp.int32, (128, 128), 0)
    earlier = (depth < lane) & ((depth < tokens) == (lane < tokens))
    earlier = jnp.where(earlier, 1.0, 0.0).astype(bf16)
    row_id = lax.broadcasted_iota(jnp.int32, (rows, 128), 0).astype(f32)
    group_row = lax.broadcasted_iota(jnp.int32, (GROUP, 128), 0).astype(f32) * CAPACITY
    group_lane = lax.broadcasted_iota(jnp.int32, (GROUP, 128), 1)

    def select(c):
        meta = ring[pl.ds(c * GROUP, GROUP), both:both + 16, :].astype(f32)
        routes = meta[:, :8, :128]
        gate = meta[:, 8:, :128] + meta[:, :8, 128:] + meta[:, 8:, 128:]
        codes, weights = [], []
        for e in range(local):
            hit = routes == (me * local + e).astype(f32)
            chosen = jnp.max(jnp.where(hit, 1.0, 0.0), axis=1)
            weights.append(jnp.sum(jnp.where(hit, gate, 0.0), axis=1))
            rank = nn_dot(chosen.astype(bf16), earlier)
            codes.append(jnp.where(chosen > 0.5, rank + group_row, -1.0))
        by_kind = [jnp.where(group_lane < tokens, code, -1.0) for code in codes]
        by_kind += [jnp.where(group_lane >= tokens, code, -1.0) for code in codes]
        total = jnp.zeros((2 * local * rows, width), f32)
        scale = [jnp.zeros((rows, 128), f32) for _ in range(local)]
        for q in range(GROUP):
            match = [row_id == code[q:q + 1, :] for code in by_kind]
            pick = jnp.concatenate([jnp.where(m, 1.0, 0.0) for m in match], axis=0).astype(bf16)
            picks[c * GROUP + q] = pick
            block = ring[c * GROUP + q]
            total = total + nn_dot(pick[:, :both + 16], block)
            for e in range(local):
                scale[e] = scale[e] + jnp.where(match[local + e], weights[e][q:q + 1, :], 0.0)
        scale = jnp.sum(jnp.concatenate(scale, axis=0), axis=1, keepdims=True)
        gates[c] = jnp.broadcast_to(scale, (local * rows, 128))
        xrows[head, c, 0] = total[: local * rows].astype(bf16).reshape(local, rows, width)
        xrows[head, c, 1] = (total[local * rows:] * scale).astype(bf16).reshape(local, rows, width)

    def gather_group(c, carry):
        for n in (1, 2):
            k = 2 * c + n
            for s in (0, 1):
                go_ahead(k, 0, s).wait_recv()

                @pl.when(k < hops)
                def _():
                    go_ahead(k + 1, 0, s).start()
                    go_behind(k, 0, s).wait_recv()

                @pl.when(k < hops - 1)
                def _():
                    go_behind(k + 1, 0, s).start()

            @pl.when(k < hops)
            def _():
                for s in (0, 1):
                    go_ahead(k + 1, 1, s).start()
                    go_behind(k + 1, 1, s).start()

        for n in (1, 2):
            for s in (0, 1):
                go_ahead(2 * c + n, 1, s).wait_recv()
                go_behind(2 * c + n, 1, s).wait_recv()
        select(c)
        for d in range(1, heads):
            spread(d, c).start()
        return carry

    lax.fori_loop(0, chunks, gather_group, 0)
    load_in.wait()
    load_out.wait()

    def spread_wait(c, carry):
        for d in range(1, heads):
            spread(d, c).wait()
        return carry

    lax.fori_loop(0, chunks, spread_wait, 0)

    def taken(kind, e, h):
        return xrows[h, :, kind, e].reshape(chunks * rows, width)

    def expert(e, carry):
        got = [jnp.concatenate([taken(k, e, h) for h in range(heads)], axis=1) for k in range(2)]
        for p in range(pieces):
            part = pl.ds(p * 256, 256)
            positive = jnp.maximum(nt_dot(got[0], win[e, part, :]), 0.0)
            acts[0, e, p] = (positive * positive).astype(bf16)
            grad = nt_dot(got[1], wout[e, part, :])
            acts[1, e, p] = (grad * 2.0 * positive).astype(bf16)
        for k, weight in ((0, wout), (1, win)):
            act = jnp.concatenate([acts[k, e, p] for p in range(pieces)], axis=1)
            for h in range(heads):
                out = nn_dot(act, weight[e, :, h * width:(h + 1) * width])
                yown[h, :, k, e] = out.astype(bf16).reshape(chunks, rows, width)
        return carry

    lax.fori_loop(0, local, expert, 0)

    def share(d, c):
        return remote(
            yown.at[head_at[d], c], yland.at[d - 1, c], os_.at[d - 1, c], or_.at[d - 1, c],
            {"head": head_at[d]},
        )

    def share_start(k, carry):
        for d in range(1, heads):
            share(d, chunks - 1 - k).start()
        return carry

    lax.fori_loop(0, chunks, share_start, 0)

    def weight_grads(e, carry):
        for p in range(pieces):
            for h in range(heads):
                for w in range(2):
                    piece = tn_dot(acts[1 - w, e, p], taken(w, e, h)).astype(bf16)
                    for s in range(width // 128):
                        dest = h * (width // 128) + s
                        parts[dest % 2, dest // 2, w, e, p * 256:(p + 1) * 256, :] = (
                            piece[:, s * 128:(s + 1) * 128]
                        )
        return carry

    lax.fori_loop(0, local, weight_grads, 0)
    pair_copy = remote(parts.at[1 - core], pair, ps.at[0], pr.at[0], sibling)
    pair_copy.start()

    def combine(c):
        for d in range(1, heads):
            share(d, c).wait_recv()
        total = yown[head, c].astype(f32)
        for d in range(1, heads):
            total = total + yland[d - 1, c].astype(f32)
        out = total[0].reshape(local * rows, width) * gates[c][:, :1]
        back = total[1].reshape(local * rows, width)
        total = jnp.concatenate([out, back], axis=0).astype(bf16)
        for q in range(GROUP):
            contrib[c * GROUP + q] = tn_dot(picks[c * GROUP + q], total)[:both].astype(bf16)

    def block_ahead(d):
        return 2 * d - jnp.where(d == half, 1, 0)

    def sum_copy(way, j, s):
        side, part = way % 2, piece_of(s, both)
        d = half - side - 2 * j
        block = block_ahead(d) if way < 2 else 2 * d - 1
        return remote(
            contrib.at[block, part], landed.at[way, j, part], rs.at[way, j, s], rr.at[way, j, s],
            (ahead if way < 2 else behind)[1 - side],
        )

    def cross_copy(d):
        return remote(
            parts.at[core, x_at[d]], cross.at[d - 1], cs.at[d - 1], cr.at[d - 1],
            {"dp": x_at[d] * 2 + core},
        )

    def sum_into(block, ways, j, s):
        part = piece_of(s, both)
        total = contrib[block, part].astype(f32)
        for way in ways:
            sum_copy(way, j, s).wait_recv()
            total = total + landed[way, j, part].astype(f32)
        contrib[block, part] = total.astype(bf16)

    def sum_group(g, carry):
        combine(chunks - 1 - g)
        for n in (0, 1):
            for s in (0, 1):
                sum_copy(1, 2 * g + n, s).start()
                sum_copy(3, 2 * g + n, s).start()
        for n in (0, 1):
            j = 2 * g + n
            d = half - 2 * j
            for s in (0, 1):

                @pl.when(j > 0)
                def _():
                    sum_into(block_ahead(d), (0, 1), j - 1, s)

                sum_copy(0, j, s).start()

                @pl.when(j == 1)
                def _():
                    sum_into(2 * d - 1, (3,), j - 1, s)

                @pl.when(j > 1)
                def _():
                    sum_into(2 * d - 1, (2, 3), j - 1, s)

                @pl.when(j > 0)
                def _():
                    sum_copy(2, j, s).start()

        @pl.when(g == 0)
        def _():
            pair_copy.wait()

            def merge(k, inner):
                x, w, e = k // (2 * local), (k // local) % 2, k % local
                parts[core, x, w, e] = (
                    parts[core, x, w, e].astype(f32) + pair[x, w, e].astype(f32)
                ).astype(bf16)
                return inner

            lax.fori_loop(0, xs * 2 * local, merge, 0)
            for d in range(1, xs):
                cross_copy(d).start()

        return carry

    lax.fori_loop(0, chunks, sum_group, 0)
    mine = contrib[0].astype(f32)
    for way in range(4):
        for s in (0, 1):
            sum_copy(way, hops - 1, s).wait_recv()
        mine = mine + landed[way, hops - 1].astype(f32)
    mine = mine.astype(bf16)
    columns = pl.ds(pl.multiple_of(head * width, width), width)
    tok_ref[:, columns] = mine

    def tell(d):
        return remote(
            tok_ref.at[:, columns], tok_ref.at[:, columns], ts.at[d - 1], tr.at[d - 1],
            {"head": head_at[d]},
        )

    for d in range(1, heads):
        tell(d).start()
    for d in range(1, xs):
        cross_copy(d).wait()

    def finish(k, carry):
        w, e = k // local, k % local
        total = parts[core, px, w, e].astype(f32)
        for d in range(1, xs):
            total = total + cross[d - 1, w, e].astype(f32)
        wgrad_ref[w, e] = total.astype(bf16)
        return carry

    lax.fori_loop(0, 2 * local, finish, 0)

    def drain_ring(k, carry):
        for s in (0, 1):
            for side in (0, 1):
                go_ahead(k, side, s).wait_send()
                sum_copy(side, k - 1, s).wait_send()
            go_behind(k, 1, s).wait_send()
            sum_copy(3, k - 1, s).wait_send()

            @pl.when(k < hops)
            def _():
                go_behind(k, 0, s).wait_send()
                sum_copy(2, k, s).wait_send()

        return carry

    lax.fori_loop(1, hops + 1, drain_ring, 0)

    def drain_share(c, carry):
        for d in range(1, heads):
            share(d, c).wait_send()
        return carry

    lax.fori_loop(0, chunks, drain_share, 0)
    for d in range(1, heads):
        tell(d).wait()


def on_device(latent, cotangent, routes, gate_values, weight_in, weight_out):
    tokens, latent_width = latent.shape
    owners = lax.axis_size("expert")
    heads = lax.axis_size("head")
    xs = lax.axis_size("dp") // 2
    local, hidden, _ = weight_in.shape
    width = latent_width // heads
    head = lax.axis_index("head")
    both = 2 * tokens
    half = owners // 2
    chunks = owners // GROUP
    rows = GROUP * CAPACITY

    data = jnp.concatenate([latent, cotangent], 0)
    data = lax.dynamic_slice(data, (0, head * width), (both, width))
    named = routes.T.astype(f32)
    gate = gate_values.T
    high = lax.reduce_precision(gate, 8, 7)
    middle = lax.reduce_precision(gate - high, 8, 7)
    low = lax.reduce_precision(gate - high - middle, 8, 7)

    def on_grads(piece):
        return jnp.pad(piece, ((0, 0), (tokens, 128 - both)))

    named = jnp.pad(
        jnp.concatenate([named, named], 1), ((0, 0), (0, 128 - both)), constant_values=-1.0
    )
    meta = jnp.concatenate(
        [
            jnp.concatenate([named, on_grads(middle)], 1),
            jnp.concatenate([on_grads(high), on_grads(low)], 1),
        ],
        0,
    )
    block = jnp.concatenate([data, meta.astype(bf16)], 0)

    dma = pltpu.SemaphoreType.DMA
    vmem = pltpu.VMEM
    tokens_out, grads_out = pl.pallas_call(
        functools.partial(kernel, (owners, heads, xs, tokens, local)),
        out_shape=(
            jax.ShapeDtypeStruct((both, latent_width), bf16),
            jax.ShapeDtypeStruct((2, local, hidden, 128), bf16),
        ),
        in_specs=[
            pl.BlockSpec(memory_space=pltpu.VMEM),
            pl.BlockSpec(memory_space=pltpu.HBM),
            pl.BlockSpec(memory_space=pltpu.HBM),
        ],
        out_specs=(
            pl.BlockSpec(memory_space=pltpu.VMEM),
            pl.BlockSpec(memory_space=pltpu.VMEM),
        ),
        scratch_shapes=[
            vmem((owners, both + 16, width), bf16),
            vmem((owners, 2 * local * rows, 128), bf16),
            vmem((chunks, local * rows, 128), f32),
            vmem((heads, chunks, 2, local, rows, width), bf16),
            vmem((local, hidden, latent_width), bf16),
            vmem((local, hidden, latent_width), bf16),
            vmem((2, local, hidden // 256, chunks * rows, 256), bf16),
            vmem((heads, chunks, 2, local, rows, width), bf16),
            vmem((heads - 1, chunks, 2, local, rows, width), bf16),
            vmem((owners, both, width), bf16),
            vmem((4, half // 2, both, width), bf16),
            vmem((2, xs, 2, local, hidden, 128), bf16),
            vmem((xs, 2, local, hidden, 128), bf16),
            vmem((xs - 1, 2, local, hidden, 128), bf16),
            dma((2,)),
            dma((2, half + 1, 2)),
            dma((2, half + 1, 2)),
            dma((heads - 1, chunks)),
            dma((heads - 1, chunks)),
            dma((heads - 1, chunks)),
            dma((heads - 1, chunks)),
            dma((4, half // 2, 2)),
            dma((4, half // 2, 2)),
            dma((1,)),
            dma((1,)),
            dma((xs - 1,)),
            dma((xs - 1,)),
            dma((heads - 1,)),
            dma((heads - 1,)),
        ],
        compiler_params=pltpu.CompilerParams(
            collective_id=0, has_side_effects=True, vmem_limit_bytes=52 * 1024 * 1024
        ),
        name="experts",
    )(block, weight_in, weight_out)
    return tokens_out[:tokens], tokens_out[tokens:], grads_out[0], grads_out[1]


def solution(mesh):
    in_specs = (
        P(("dp", "expert"), None),
        P(("dp", "expert"), None),
        P(("dp", "expert"), None),
        P(("dp", "expert"), None),
        P("expert", "head", None),
        P("expert", "head", None),
    )
    out_specs = (
        P(("dp", "expert"), None),
        P(("dp", "expert"), None),
        P("expert", "head", "dp"),
        P("expert", "head", "dp"),
    )
    return jax.shard_map(
        on_device, mesh=mesh, in_specs=in_specs, out_specs=out_specs, check_vma=False
    )
```

```python
import functools

import jax
import jax.numpy as jnp
from jax import lax
from jax.experimental import pallas as pl
from jax.experimental.pallas import tpu as pltpu
from jax.sharding import PartitionSpec as P

CAPACITY = 6
GROUP = 8
MESH = pl.DeviceIdType.MESH
f32, bf16 = jnp.float32, jnp.bfloat16


def nt_dot(a, b):
    return lax.dot_general(a, b, (((1,), (1,)), ((), ())), preferred_element_type=f32)


def nn_dot(a, b):
    return lax.dot_general(a, b, (((1,), (0,)), ((), ())), preferred_element_type=f32)


def tn_dot(a, b):
    return lax.dot_general(a, b, (((0,), (0,)), ((), ())), preferred_element_type=f32)


def kernel(
    dims, latent_hbm, cotangent_hbm, routes_hbm, gate_hbm, win_hbm, wout_hbm,
    moe_ref, back_ref, in_grad_hbm, out_grad_hbm, tok_ref, latent_ref, cotangent_ref, routes_ref, gate_ref, wgrad_ref, ring, picks, gates, xrows, win, wout, acts, yown, yland, contrib, landed,
    parts, pair, cross,
    w_sem, zs, zr, ys, yr, os_, or_, rs, rr, ps, pr, cs, cr, ts, tr,
):
    owners, heads, xs, tokens, local = dims
    half = owners // 2
    hops = half // 2
    chunks = owners // GROUP
    rows = GROUP * CAPACITY
    both = 2 * tokens
    width = ring.shape[2]
    hidden = win.shape[1]
    pieces = hidden // 256

    me = lax.axis_index("expert")
    head = lax.axis_index("head")
    dp = lax.axis_index("dp")
    px, core = dp // 2, dp % 2
    ahead = [{"expert": lax.rem(me + d, owners)} for d in (1, 2)]
    behind = [{"expert": lax.rem(me + owners - d, owners)} for d in (1, 2)]
    head_at = [lax.rem(head + d, heads) for d in range(heads)]
    x_at = [lax.rem(px + d, xs) for d in range(xs)]
    sibling = {"dp": px * 2 + 1 - core}

    def remote(src, dst, send, recv, device):
        return pltpu.make_async_remote_copy(
            src_ref=src, dst_ref=dst, send_sem=send, recv_sem=recv,
            device_id=device, device_id_type=MESH,
        )

    small = [
        pltpu.make_async_copy(src, dst, w_sem.at[2 + i])
        for i, (src, dst) in enumerate(
            [
                (latent_hbm, latent_ref),
                (cotangent_hbm, cotangent_ref),
                (routes_hbm, routes_ref),
                (gate_hbm, gate_ref),
            ]
        )
    ]
    for copy in small:
        copy.start()
    load_in = pltpu.make_async_copy(win_hbm, win, w_sem.at[0])
    load_out = pltpu.make_async_copy(wout_hbm, wout, w_sem.at[1])

    barrier = pltpu.get_barrier_semaphore()
    partners = ahead + behind + [sibling]
    partners += [{"head": head_at[d]} for d in range(1, heads)]
    partners += [{"dp": x_at[d] * 2 + core} for d in range(1, xs)]
    for device in partners:
        pl.semaphore_signal(barrier, inc=1, device_id=device, device_id_type=MESH)

    load_in.start()
    load_out.start()
    for copy in small:
        copy.wait()
    columns = pl.ds(pl.multiple_of(head * width, width), width)
    own = [latent_ref[:, columns].astype(f32), cotangent_ref[:, columns].astype(f32)]
    ring[0, :both] = jnp.concatenate(own, axis=0).astype(bf16)
    token_id = lax.broadcasted_iota(jnp.int32, (tokens, 128), 0)
    lane_id = lax.broadcasted_iota(jnp.int32, (tokens, 128), 1)
    on_grads = lane_id == token_id + tokens
    on_rows = lane_id == token_id
    spare = lax.broadcasted_iota(jnp.int32, (8, 128), 1) >= both
    twice = jnp.where(on_rows | on_grads, 1.0, 0.0).astype(bf16)
    once = jnp.where(on_grads, 1.0, 0.0).astype(bf16)
    named = nn_dot(routes_ref[...].astype(f32).astype(bf16), twice)
    named = jnp.where(spare, -1.0, named)
    rest = gate_ref[...]
    pieces_of_gate = []
    for _ in range(3):
        piece = rest.astype(bf16)
        pieces_of_gate.append(nn_dot(piece, once))
        rest = rest - piece.astype(f32)
    high, middle, low = pieces_of_gate
    top = jnp.concatenate([named, middle], axis=1)
    bottom = jnp.concatenate([high, low], axis=1)
    ring[0, both:] = jnp.concatenate([top, bottom], axis=0).astype(bf16)
    pl.semaphore_wait(barrier, len(partners))

    def slot_ahead(d):
        return jnp.maximum(2 * d - 1, 0)

    def piece_of(s, total):
        return pl.ds(0, 48) if s == 0 else pl.ds(48, total - 48)

    def go_ahead(k, side, s):
        to, part = 2 * k - side, piece_of(s, both + 16)
        return remote(
            ring.at[slot_ahead(2 * k - 2), part], ring.at[slot_ahead(to), part],
            zs.at[0, to, s], zr.at[0, to, s], ahead[1 - side],
        )

    def go_behind(k, side, s):
        to, part = 2 * k - side, piece_of(s, both + 16)
        return remote(
            ring.at[2 * (2 * k - 2), part], ring.at[2 * to, part],
            zs.at[1, to, s], zr.at[1, to, s], behind[1 - side],
        )

    def spread(d, c):
        return remote(
            xrows.at[head, c], xrows.at[head, c], ys.at[d - 1, c], yr.at[d - 1, c],
            {"head": head_at[d]},
        )

    for side in (0, 1):
        for s in (0, 1):
            go_ahead(1, side, s).start()
            go_behind(1, side, s).start()

    lane = lax.broadcasted_iota(jnp.int32, (128, 128), 1)
    depth = lax.broadcasted_iota(jnp.int32, (128, 128), 0)
    earlier = (depth < lane) & ((depth < tokens) == (lane < tokens))
    earlier = jnp.where(earlier, 1.0, 0.0).astype(bf16)
    row_id = lax.broadcasted_iota(jnp.int32, (rows, 128), 0).astype(f32)
    group_row = lax.broadcasted_iota(jnp.int32, (GROUP, 128), 0).astype(f32) * CAPACITY
    group_lane = lax.broadcasted_iota(jnp.int32, (GROUP, 128), 1)

    def select(c):
        meta = ring[pl.ds(c * GROUP, GROUP), both:both + 16, :].astype(f32)
        routes = meta[:, :8, :128]
        gate = meta[:, 8:, :128] + meta[:, :8, 128:] + meta[:, 8:, 128:]
        codes, weights = [], []
        for e in range(local):
            hit = routes == (me * local + e).astype(f32)
            chosen = jnp.max(jnp.where(hit, 1.0, 0.0), axis=1)
            weights.append(jnp.sum(jnp.where(hit, gate, 0.0), axis=1))
            rank = nn_dot(chosen.astype(bf16), earlier)
            codes.append(jnp.where(chosen > 0.5, rank + group_row, -1.0))
        by_kind = [jnp.where(group_lane < tokens, code, -1.0) for code in codes]
        by_kind += [jnp.where(group_lane >= tokens, code, -1.0) for code in codes]
        total = jnp.zeros((2 * local * rows, width), f32)
        scale = [jnp.zeros((rows, 128), f32) for _ in range(local)]
        for q in range(GROUP):
            match = [row_id == code[q:q + 1, :] for code in by_kind]
            pick = jnp.concatenate([jnp.where(m, 1.0, 0.0) for m in match], axis=0).astype(bf16)
            picks[c * GROUP + q] = pick
            block = ring[c * GROUP + q]
            total = total + nn_dot(pick[:, :both + 16], block)
            for e in range(local):
                scale[e] = scale[e] + jnp.where(match[local + e], weights[e][q:q + 1, :], 0.0)
        scale = jnp.sum(jnp.concatenate(scale, axis=0), axis=1, keepdims=True)
        gates[c] = jnp.broadcast_to(scale, (local * rows, 128))
        xrows[head, c, 0] = total[: local * rows].astype(bf16).reshape(local, rows, width)
        xrows[head, c, 1] = (total[local * rows:] * scale).astype(bf16).reshape(local, rows, width)

    def gather_group(c, carry):
        for n in (1, 2):
            k = 2 * c + n
            for s in (0, 1):
                go_ahead(k, 0, s).wait_recv()

                @pl.when(k < hops)
                def _():
                    go_ahead(k + 1, 0, s).start()
                    go_behind(k, 0, s).wait_recv()

                @pl.when(k < hops - 1)
                def _():
                    go_behind(k + 1, 0, s).start()

            @pl.when(k < hops)
            def _():
                for s in (0, 1):
                    go_ahead(k + 1, 1, s).start()
                    go_behind(k + 1, 1, s).start()

        for n in (1, 2):
            for s in (0, 1):
                go_ahead(2 * c + n, 1, s).wait_recv()
                go_behind(2 * c + n, 1, s).wait_recv()
        select(c)
        for d in range(1, heads):
            spread(d, c).start()
        return carry

    lax.fori_loop(0, chunks, gather_group, 0)
    load_in.wait()
    load_out.wait()

    def spread_wait(c, carry):
        for d in range(1, heads):
            spread(d, c).wait()
        return carry

    lax.fori_loop(0, chunks, spread_wait, 0)

    def taken(kind, e, h):
        return xrows[h, :, kind, e].reshape(chunks * rows, width)

    def share(d, c, e):
        return remote(
            yown.at[head_at[d], c, e], yland.at[d - 1, c, e],
            os_.at[d - 1, c, e], or_.at[d - 1, c, e], {"head": head_at[d]},
        )

    def expert(e, carry):
        got = [jnp.concatenate([taken(k, e, h) for h in range(heads)], axis=1) for k in range(2)]
        for p in range(pieces):
            part = pl.ds(p * 256, 256)
            positive = jnp.maximum(nt_dot(got[0], win[e, part, :]), 0.0)
            acts[0, e, p] = (positive * positive).astype(bf16)
            grad = nt_dot(got[1], wout[e, part, :])
            acts[1, e, p] = (grad * 2.0 * positive).astype(bf16)
        for k, weight in ((0, wout), (1, win)):
            act = jnp.concatenate([acts[k, e, p] for p in range(pieces)], axis=1)
            for h in range(heads):
                out = nn_dot(act, weight[e, :, h * width:(h + 1) * width])
                yown[h, :, e, k] = out.astype(bf16).reshape(chunks, rows, width)
        for d in range(1, heads):
            share(d, chunks - 1, e).start()
        return carry

    lax.fori_loop(0, local, expert, 0)

    def share_start(k, carry):
        for e in range(local):
            for d in range(1, heads):
                share(d, chunks - 1 - k, e).start()
        return carry

    lax.fori_loop(1, chunks, share_start, 0)

    def weight_grads(e, carry):
        for p in range(pieces):
            for h in range(heads):
                for w in range(2):
                    piece = tn_dot(acts[1 - w, e, p], taken(w, e, h)).astype(bf16)
                    for s in range(width // 128):
                        dest = h * (width // 128) + s
                        parts[dest % 2, dest // 2, w, e, p * 256:(p + 1) * 256, :] = (
                            piece[:, s * 128:(s + 1) * 128]
                        )
        return carry

    lax.fori_loop(0, local, weight_grads, 0)
    pair_copy = remote(parts.at[1 - core], pair, ps.at[0], pr.at[0], sibling)
    pair_copy.start()

    def combine(c):
        for d in range(1, heads):
            for e in range(local):
                share(d, c, e).wait_recv()
        total = yown[head, c].astype(f32)
        for d in range(1, heads):
            total = total + yland[d - 1, c].astype(f32)
        scale = gates[c][:, :1]
        out = [total[e, 0] * scale[e * rows:(e + 1) * rows] for e in range(local)]
        back = [total[e, 1] for e in range(local)]
        total = jnp.concatenate(out + back, axis=0).astype(bf16)
        for q in range(GROUP):
            contrib[c * GROUP + q] = tn_dot(picks[c * GROUP + q], total)[:both].astype(bf16)

    def block_ahead(d):
        return 2 * d - jnp.where(d == half, 1, 0)

    def sum_copy(way, j, s):
        side, part = way % 2, piece_of(s, both)
        d = half - side - 2 * j
        block = block_ahead(d) if way < 2 else 2 * d - 1
        return remote(
            contrib.at[block, part], landed.at[way, j, part], rs.at[way, j, s], rr.at[way, j, s],
            (ahead if way < 2 else behind)[1 - side],
        )

    def cross_copy(d):
        return remote(
            parts.at[core, x_at[d]], cross.at[d - 1], cs.at[d - 1], cr.at[d - 1],
            {"dp": x_at[d] * 2 + core},
        )

    def sum_into(block, ways, j, s):
        part = piece_of(s, both)
        total = contrib[block, part].astype(f32)
        for way in ways:
            sum_copy(way, j, s).wait_recv()
            total = total + landed[way, j, part].astype(f32)
        contrib[block, part] = total.astype(bf16)

    def sum_group(g, carry):
        combine(chunks - 1 - g)
        for n in (0, 1):
            for s in (0, 1):
                sum_copy(1, 2 * g + n, s).start()
                sum_copy(3, 2 * g + n, s).start()
        for n in (0, 1):
            j = 2 * g + n
            d = half - 2 * j
            for s in (0, 1):

                @pl.when(j > 0)
                def _():
                    sum_into(block_ahead(d), (0, 1), j - 1, s)

                sum_copy(0, j, s).start()

                @pl.when(j == 1)
                def _():
                    sum_into(2 * d - 1, (3,), j - 1, s)

                @pl.when(j > 1)
                def _():
                    sum_into(2 * d - 1, (2, 3), j - 1, s)

                @pl.when(j > 0)
                def _():
                    sum_copy(2, j, s).start()

        @pl.when(g == 0)
        def _():
            pair_copy.wait()

            def merge(k, inner):
                x, w, e = k // (2 * local), (k // local) % 2, k % local
                parts[core, x, w, e] = (
                    parts[core, x, w, e].astype(f32) + pair[x, w, e].astype(f32)
                ).astype(bf16)
                return inner

            lax.fori_loop(0, xs * 2 * local, merge, 0)
            for d in range(1, xs):
                cross_copy(d).start()

        return carry

    lax.fori_loop(0, chunks, sum_group, 0)
    mine = contrib[0].astype(f32)
    for way in range(4):
        for s in (0, 1):
            sum_copy(way, hops - 1, s).wait_recv()
        mine = mine + landed[way, hops - 1].astype(f32)
    mine = mine.astype(bf16)
    tok_ref[:, columns] = mine

    def tell(d):
        return remote(
            tok_ref.at[:, columns], tok_ref.at[:, columns], ts.at[d - 1], tr.at[d - 1],
            {"head": head_at[d]},
        )

    for d in range(1, heads):
        tell(d).start()
    for d in range(1, xs):
        cross_copy(d).wait()

    def finish(k, carry):
        w, e = k // local, k % local
        total = parts[core, px, w, e].astype(f32)
        for d in range(1, xs):
            total = total + cross[d - 1, w, e].astype(f32)
        wgrad_ref[w, e] = total.astype(bf16)
        return carry

    lax.fori_loop(0, 2 * local, finish, 0)
    stores = [
        pltpu.make_async_copy(wgrad_ref.at[0], in_grad_hbm, w_sem.at[6]),
        pltpu.make_async_copy(wgrad_ref.at[1], out_grad_hbm, w_sem.at[7]),
    ]
    for copy in stores:
        copy.start()

    def drain_ring(k, carry):
        for s in (0, 1):
            for side in (0, 1):
                go_ahead(k, side, s).wait_send()
                sum_copy(side, k - 1, s).wait_send()
            go_behind(k, 1, s).wait_send()
            sum_copy(3, k - 1, s).wait_send()

            @pl.when(k < hops)
            def _():
                go_behind(k, 0, s).wait_send()
                sum_copy(2, k, s).wait_send()

        return carry

    lax.fori_loop(1, hops + 1, drain_ring, 0)

    def drain_share(c, carry):
        for d in range(1, heads):
            for e in range(local):
                share(d, c, e).wait_send()
        return carry

    lax.fori_loop(0, chunks, drain_share, 0)
    for d in range(1, heads):
        tell(d).wait()
    whole = tok_ref[...].astype(f32)
    moe_ref[...] = whole[:tokens].astype(bf16)
    back_ref[...] = whole[tokens:].astype(bf16)
    for copy in stores:
        copy.wait()


def on_device(latent, cotangent, routes, gate_values, weight_in, weight_out):
    tokens, latent_width = latent.shape
    owners = lax.axis_size("expert")
    heads = lax.axis_size("head")
    xs = lax.axis_size("dp") // 2
    local, hidden, _ = weight_in.shape
    width = latent_width // heads
    both = 2 * tokens
    half = owners // 2
    chunks = owners // GROUP
    rows = GROUP * CAPACITY

    dma = pltpu.SemaphoreType.DMA
    vmem = pltpu.VMEM
    return pl.pallas_call(
        functools.partial(kernel, (owners, heads, xs, tokens, local)),
        out_shape=(
            jax.ShapeDtypeStruct((tokens, latent_width), bf16),
            jax.ShapeDtypeStruct((tokens, latent_width), bf16),
            jax.ShapeDtypeStruct((local, hidden, 128), bf16),
            jax.ShapeDtypeStruct((local, hidden, 128), bf16),
        ),
        in_specs=[
            pl.BlockSpec(memory_space=pltpu.HBM),
            pl.BlockSpec(memory_space=pltpu.HBM),
            pl.BlockSpec(memory_space=pltpu.HBM),
            pl.BlockSpec(memory_space=pltpu.HBM),
            pl.BlockSpec(memory_space=pltpu.HBM),
            pl.BlockSpec(memory_space=pltpu.HBM),
        ],
        out_specs=(
            pl.BlockSpec(memory_space=pltpu.VMEM),
            pl.BlockSpec(memory_space=pltpu.VMEM),
            pl.BlockSpec(memory_space=pltpu.HBM),
            pl.BlockSpec(memory_space=pltpu.HBM),
        ),
        scratch_shapes=[
            vmem((both, latent_width), bf16),
            vmem((tokens, latent_width), bf16),
            vmem((tokens, latent_width), bf16),
            vmem(routes.T.shape, jnp.int32),
            vmem(routes.T.shape, f32),
            vmem((2, local, hidden, 128), bf16),
            vmem((owners, both + 16, width), bf16),
            vmem((owners, 2 * local * rows, 128), bf16),
            vmem((chunks, local * rows, 128), f32),
            vmem((heads, chunks, 2, local, rows, width), bf16),
            vmem((local, hidden, latent_width), bf16),
            vmem((local, hidden, latent_width), bf16),
            vmem((2, local, hidden // 256, chunks * rows, 256), bf16),
            vmem((heads, chunks, local, 2, rows, width), bf16),
            vmem((heads - 1, chunks, local, 2, rows, width), bf16),
            vmem((owners, both, width), bf16),
            vmem((4, half // 2, both, width), bf16),
            vmem((2, xs, 2, local, hidden, 128), bf16),
            vmem((xs, 2, local, hidden, 128), bf16),
            vmem((xs - 1, 2, local, hidden, 128), bf16),
            dma((8,)),
            dma((2, half + 1, 2)),
            dma((2, half + 1, 2)),
            dma((heads - 1, chunks)),
            dma((heads - 1, chunks)),
            dma((heads - 1, chunks, local)),
            dma((heads - 1, chunks, local)),
            dma((4, half // 2, 2)),
            dma((4, half // 2, 2)),
            dma((1,)),
            dma((1,)),
            dma((xs - 1,)),
            dma((xs - 1,)),
            dma((heads - 1,)),
            dma((heads - 1,)),
        ],
        compiler_params=pltpu.CompilerParams(
            collective_id=0, has_side_effects=True, vmem_limit_bytes=60 * 1024 * 1024
        ),
        name="experts",
    )(latent, cotangent, routes.T, gate_values.T, weight_in, weight_out)


def solution(mesh):
    in_specs = (
        P(("dp", "expert"), None),
        P(("dp", "expert"), None),
        P(("dp", "expert"), None),
        P(("dp", "expert"), None),
        P("expert", "head", None),
        P("expert", "head", None),
    )
    out_specs = (
        P(("dp", "expert"), None),
        P(("dp", "expert"), None),
        P("expert", "head", "dp"),
        P("expert", "head", "dp"),
    )
    return jax.shard_map(
        on_device, mesh=mesh, in_specs=in_specs, out_specs=out_specs, check_vma=False
    )
```

```python
import functools

import jax
import jax.numpy as jnp
from jax import lax
from jax.experimental import pallas as pl
from jax.experimental.pallas import tpu as pltpu
from jax.sharding import PartitionSpec as P

CAPACITY = 6
GROUP = 8
MESH = pl.DeviceIdType.MESH
f32, bf16 = jnp.float32, jnp.bfloat16


def nt_dot(a, b):
    return lax.dot_general(a, b, (((1,), (1,)), ((), ())), preferred_element_type=f32)


def nn_dot(a, b):
    return lax.dot_general(a, b, (((1,), (0,)), ((), ())), preferred_element_type=f32)


def tn_dot(a, b):
    return lax.dot_general(a, b, (((0,), (0,)), ((), ())), preferred_element_type=f32)


def kernel(
    dims, blk_ref, win_hbm, wout_hbm, tok_ref, wgrad_ref,
    ring, picks, gates, xrows, win, wout, acts, yown, yland, contrib, landed,
    parts, pair, cross,
    w_sem, zs, zr, ys, yr, os_, or_, rs, rr, ps, pr, cs, cr, ts, tr,
):
    owners, heads, xs, tokens, local = dims
    half = owners // 2
    hops = half // 2
    chunks = owners // GROUP
    rows = GROUP * CAPACITY
    both = 2 * tokens
    width = ring.shape[2]
    hidden = win.shape[1]
    pieces = hidden // 256

    me = lax.axis_index("expert")
    head = lax.axis_index("head")
    dp = lax.axis_index("dp")
    px, core = dp // 2, dp % 2
    ahead = [{"expert": lax.rem(me + d, owners)} for d in (1, 2)]
    behind = [{"expert": lax.rem(me + owners - d, owners)} for d in (1, 2)]
    head_at = [lax.rem(head + d, heads) for d in range(heads)]
    x_at = [lax.rem(px + d, xs) for d in range(xs)]
    sibling = {"dp": px * 2 + 1 - core}

    def remote(src, dst, send, recv, device):
        return pltpu.make_async_remote_copy(
            src_ref=src, dst_ref=dst, send_sem=send, recv_sem=recv,
            device_id=device, device_id_type=MESH,
        )

    load_in = pltpu.make_async_copy(win_hbm, win, w_sem.at[0])
    load_out = pltpu.make_async_copy(wout_hbm, wout, w_sem.at[1])
    load_in.start()
    load_out.start()
    ring[0] = blk_ref[...]

    barrier = pltpu.get_barrier_semaphore()
    partners = ahead + behind + [sibling]
    partners += [{"head": head_at[d]} for d in range(1, heads)]
    partners += [{"dp": x_at[d] * 2 + core} for d in range(1, xs)]
    for device in partners:
        pl.semaphore_signal(barrier, inc=1, device_id=device, device_id_type=MESH)
    pl.semaphore_wait(barrier, len(partners))

    def slot_ahead(d):
        return jnp.maximum(2 * d - 1, 0)

    def piece_of(s, total):
        return pl.ds(0, 48) if s == 0 else pl.ds(48, total - 48)

    def go_ahead(k, side, s):
        to, part = 2 * k - side, piece_of(s, both + 16)
        return remote(
            ring.at[slot_ahead(2 * k - 2), part], ring.at[slot_ahead(to), part],
            zs.at[0, to, s], zr.at[0, to, s], ahead[1 - side],
        )

    def go_behind(k, side, s):
        to, part = 2 * k - side, piece_of(s, both + 16)
        return remote(
            ring.at[2 * (2 * k - 2), part], ring.at[2 * to, part],
            zs.at[1, to, s], zr.at[1, to, s], behind[1 - side],
        )

    def spread(d, c):
        return remote(
            xrows.at[head, c], xrows.at[head, c], ys.at[d - 1, c], yr.at[d - 1, c],
            {"head": head_at[d]},
        )

    for side in (0, 1):
        for s in (0, 1):
            go_ahead(1, side, s).start()
            go_behind(1, side, s).start()

    lane = lax.broadcasted_iota(jnp.int32, (128, 128), 1)
    depth = lax.broadcasted_iota(jnp.int32, (128, 128), 0)
    earlier = (depth < lane) & ((depth < tokens) == (lane < tokens))
    earlier = jnp.where(earlier, 1.0, 0.0).astype(bf16)
    row_id = lax.broadcasted_iota(jnp.int32, (rows, 128), 0).astype(f32)
    group_row = lax.broadcasted_iota(jnp.int32, (GROUP, 128), 0).astype(f32) * CAPACITY
    group_lane = lax.broadcasted_iota(jnp.int32, (GROUP, 128), 1)

    def select(c):
        meta = ring[pl.ds(c * GROUP, GROUP), both:both + 16, :].astype(f32)
        routes = meta[:, :8, :128]
        gate = meta[:, 8:, :128] + meta[:, :8, 128:] + meta[:, 8:, 128:]
        codes, weights = [], []
        for e in range(local):
            hit = routes == (me * local + e).astype(f32)
            chosen = jnp.max(jnp.where(hit, 1.0, 0.0), axis=1)
            weights.append(jnp.sum(jnp.where(hit, gate, 0.0), axis=1))
            rank = nn_dot(chosen.astype(bf16), earlier)
            codes.append(jnp.where(chosen > 0.5, rank + group_row, -1.0))
        by_kind = [jnp.where(group_lane < tokens, code, -1.0) for code in codes]
        by_kind += [jnp.where(group_lane >= tokens, code, -1.0) for code in codes]
        total = jnp.zeros((2 * local * rows, width), f32)
        scale = [jnp.zeros((rows, 128), f32) for _ in range(local)]
        for q in range(GROUP):
            match = [row_id == code[q:q + 1, :] for code in by_kind]
            pick = jnp.concatenate([jnp.where(m, 1.0, 0.0) for m in match], axis=0).astype(bf16)
            picks[c * GROUP + q] = pick
            block = ring[c * GROUP + q]
            total = total + nn_dot(pick[:, :both + 16], block)
            for e in range(local):
                scale[e] = scale[e] + jnp.where(match[local + e], weights[e][q:q + 1, :], 0.0)
        scale = jnp.sum(jnp.concatenate(scale, axis=0), axis=1, keepdims=True)
        gates[c] = jnp.broadcast_to(scale, (local * rows, 128))
        xrows[head, c, 0] = total[: local * rows].astype(bf16).reshape(local, rows, width)
        xrows[head, c, 1] = (total[local * rows:] * scale).astype(bf16).reshape(local, rows, width)

    def gather_group(c, carry):
        for n in (1, 2):
            k = 2 * c + n
            for s in (0, 1):
                go_ahead(k, 0, s).wait_recv()

                @pl.when(k < hops)
                def _():
                    go_ahead(k + 1, 0, s).start()
                    go_behind(k, 0, s).wait_recv()

                @pl.when(k < hops - 1)
                def _():
                    go_behind(k + 1, 0, s).start()

            @pl.when(k < hops)
            def _():
                for s in (0, 1):
                    go_ahead(k + 1, 1, s).start()
                    go_behind(k + 1, 1, s).start()

        for n in (1, 2):
            for s in (0, 1):
                go_ahead(2 * c + n, 1, s).wait_recv()
                go_behind(2 * c + n, 1, s).wait_recv()
        select(c)
        for d in range(1, heads):
            spread(d, c).start()
        return carry

    lax.fori_loop(0, chunks, gather_group, 0)
    load_in.wait()
    load_out.wait()

    def spread_wait(c, carry):
        for d in range(1, heads):
            spread(d, c).wait()
        return carry

    lax.fori_loop(0, chunks, spread_wait, 0)

    def taken(kind, e, h):
        return xrows[h, :, kind, e].reshape(chunks * rows, width)

    def share(d, c, e):
        return remote(
            yown.at[head_at[d], c, e], yland.at[d - 1, c, e],
            os_.at[d - 1, c, e], or_.at[d - 1, c, e], {"head": head_at[d]},
        )

    def expert(e, carry):
        got = [jnp.concatenate([taken(k, e, h) for h in range(heads)], axis=1) for k in range(2)]
        for p in range(pieces):
            part = pl.ds(p * 256, 256)
            positive = jnp.maximum(nt_dot(got[0], win[e, part, :]), 0.0)
            acts[0, e, p] = (positive * positive).astype(bf16)
            grad = nt_dot(got[1], wout[e, part, :])
            acts[1, e, p] = (grad * 2.0 * positive).astype(bf16)
        for k, weight in ((0, wout), (1, win)):
            act = jnp.concatenate([acts[k, e, p] for p in range(pieces)], axis=1)
            for h in range(heads):
                out = nn_dot(act, weight[e, :, h * width:(h + 1) * width])
                yown[h, :, e, k] = out.astype(bf16).reshape(chunks, rows, width)
        for d in range(1, heads):
            share(d, chunks - 1, e).start()
        return carry

    lax.fori_loop(0, local, expert, 0)

    def share_start(k, carry):
        for e in range(local):
            for d in range(1, heads):
                share(d, chunks - 1 - k, e).start()
        return carry

    lax.fori_loop(1, chunks, share_start, 0)

    def weight_grads(e, carry):
        for p in range(pieces):
            for h in range(heads):
                for w in range(2):
                    piece = tn_dot(acts[1 - w, e, p], taken(w, e, h)).astype(bf16)
                    for s in range(width // 128):
                        dest = h * (width // 128) + s
                        parts[dest % 2, dest // 2, w, e, p * 256:(p + 1) * 256, :] = (
                            piece[:, s * 128:(s + 1) * 128]
                        )
        return carry

    lax.fori_loop(0, local, weight_grads, 0)
    pair_copy = remote(parts.at[1 - core], pair, ps.at[0], pr.at[0], sibling)
    pair_copy.start()

    def combine(c):
        for d in range(1, heads):
            for e in range(local):
                share(d, c, e).wait_recv()
        total = yown[head, c].astype(f32)
        for d in range(1, heads):
            total = total + yland[d - 1, c].astype(f32)
        scale = gates[c][:, :1]
        out = [total[e, 0] * scale[e * rows:(e + 1) * rows] for e in range(local)]
        back = [total[e, 1] for e in range(local)]
        total = jnp.concatenate(out + back, axis=0).astype(bf16)
        for q in range(GROUP):
            contrib[c * GROUP + q] = tn_dot(picks[c * GROUP + q], total)[:both].astype(bf16)

    def block_ahead(d):
        return 2 * d - jnp.where(d == half, 1, 0)

    def sum_copy(way, j, s):
        side, part = way % 2, piece_of(s, both)
        d = half - side - 2 * j
        block = block_ahead(d) if way < 2 else 2 * d - 1
        return remote(
            contrib.at[block, part], landed.at[way, j, part], rs.at[way, j, s], rr.at[way, j, s],
            (ahead if way < 2 else behind)[1 - side],
        )

    def cross_copy(d):
        return remote(
            parts.at[core, x_at[d]], cross.at[d - 1], cs.at[d - 1], cr.at[d - 1],
            {"dp": x_at[d] * 2 + core},
        )

    def sum_into(block, ways, j, s):
        part = piece_of(s, both)
        total = contrib[block, part].astype(f32)
        for way in ways:
            sum_copy(way, j, s).wait_recv()
            total = total + landed[way, j, part].astype(f32)
        contrib[block, part] = total.astype(bf16)

    def sum_group(g, carry):
        combine(chunks - 1 - g)
        for n in (0, 1):
            for s in (0, 1):
                sum_copy(1, 2 * g + n, s).start()
                sum_copy(3, 2 * g + n, s).start()
        for n in (0, 1):
            j = 2 * g + n
            d = half - 2 * j
            for s in (0, 1):

                @pl.when(j > 0)
                def _():
                    sum_into(block_ahead(d), (0, 1), j - 1, s)

                sum_copy(0, j, s).start()

                @pl.when(j == 1)
                def _():
                    sum_into(2 * d - 1, (3,), j - 1, s)

                @pl.when(j > 1)
                def _():
                    sum_into(2 * d - 1, (2, 3), j - 1, s)

                @pl.when(j > 0)
                def _():
                    sum_copy(2, j, s).start()

        @pl.when(g == 0)
        def _():
            pair_copy.wait()

            def merge(k, inner):
                x, w, e = k // (2 * local), (k // local) % 2, k % local
                parts[core, x, w, e] = (
                    parts[core, x, w, e].astype(f32) + pair[x, w, e].astype(f32)
                ).astype(bf16)
                return inner

            lax.fori_loop(0, xs * 2 * local, merge, 0)
            for d in range(1, xs):
                cross_copy(d).start()

        return carry

    lax.fori_loop(0, chunks, sum_group, 0)
    mine = contrib[0].astype(f32)
    for way in range(4):
        for s in (0, 1):
            sum_copy(way, hops - 1, s).wait_recv()
        mine = mine + landed[way, hops - 1].astype(f32)
    mine = mine.astype(bf16)
    columns = pl.ds(pl.multiple_of(head * width, width), width)
    tok_ref[:, columns] = mine

    def tell(d):
        return remote(
            tok_ref.at[:, columns], tok_ref.at[:, columns], ts.at[d - 1], tr.at[d - 1],
            {"head": head_at[d]},
        )

    for d in range(1, heads):
        tell(d).start()
    for d in range(1, xs):
        cross_copy(d).wait()

    def finish(k, carry):
        w, e = k // local, k % local
        total = parts[core, px, w, e].astype(f32)
        for d in range(1, xs):
            total = total + cross[d - 1, w, e].astype(f32)
        wgrad_ref[w, e] = total.astype(bf16)
        return carry

    lax.fori_loop(0, 2 * local, finish, 0)

    def drain_ring(k, carry):
        for s in (0, 1):
            for side in (0, 1):
                go_ahead(k, side, s).wait_send()
                sum_copy(side, k - 1, s).wait_send()
            go_behind(k, 1, s).wait_send()
            sum_copy(3, k - 1, s).wait_send()

            @pl.when(k < hops)
            def _():
                go_behind(k, 0, s).wait_send()
                sum_copy(2, k, s).wait_send()

        return carry

    lax.fori_loop(1, hops + 1, drain_ring, 0)

    def drain_share(c, carry):
        for d in range(1, heads):
            for e in range(local):
                share(d, c, e).wait_send()
        return carry

    lax.fori_loop(0, chunks, drain_share, 0)
    for d in range(1, heads):
        tell(d).wait()


def on_device(latent, cotangent, routes, gate_values, weight_in, weight_out):
    tokens, latent_width = latent.shape
    owners = lax.axis_size("expert")
    heads = lax.axis_size("head")
    xs = lax.axis_size("dp") // 2
    local, hidden, _ = weight_in.shape
    width = latent_width // heads
    head = lax.axis_index("head")
    both = 2 * tokens
    half = owners // 2
    chunks = owners // GROUP
    rows = GROUP * CAPACITY

    data = jnp.concatenate([latent, cotangent], 0)
    data = lax.dynamic_slice(data, (0, head * width), (both, width))
    named = routes.T.astype(f32)
    gate = gate_values.T
    high = lax.reduce_precision(gate, 8, 7)
    middle = lax.reduce_precision(gate - high, 8, 7)
    low = lax.reduce_precision(gate - high - middle, 8, 7)

    def on_grads(piece):
        return jnp.pad(piece, ((0, 0), (tokens, 128 - both)))

    named = jnp.pad(
        jnp.concatenate([named, named], 1), ((0, 0), (0, 128 - both)), constant_values=-1.0
    )
    meta = jnp.concatenate(
        [
            jnp.concatenate([named, on_grads(middle)], 1),
            jnp.concatenate([on_grads(high), on_grads(low)], 1),
        ],
        0,
    )
    block = jnp.concatenate([data, meta.astype(bf16)], 0)

    dma = pltpu.SemaphoreType.DMA
    vmem = pltpu.VMEM
    tokens_out, grads_out = pl.pallas_call(
        functools.partial(kernel, (owners, heads, xs, tokens, local)),
        out_shape=(
            jax.ShapeDtypeStruct((both, latent_width), bf16),
            jax.ShapeDtypeStruct((2, local, hidden, 128), bf16),
        ),
        in_specs=[
            pl.BlockSpec(memory_space=pltpu.VMEM),
            pl.BlockSpec(memory_space=pltpu.HBM),
            pl.BlockSpec(memory_space=pltpu.HBM),
        ],
        out_specs=(
            pl.BlockSpec(memory_space=pltpu.VMEM),
            pl.BlockSpec(memory_space=pltpu.VMEM),
        ),
        scratch_shapes=[
            vmem((owners, both + 16, width), bf16),
            vmem((owners, 2 * local * rows, 128), bf16),
            vmem((chunks, local * rows, 128), f32),
            vmem((heads, chunks, 2, local, rows, width), bf16),
            vmem((local, hidden, latent_width), bf16),
            vmem((local, hidden, latent_width), bf16),
            vmem((2, local, hidden // 256, chunks * rows, 256), bf16),
            vmem((heads, chunks, local, 2, rows, width), bf16),
            vmem((heads - 1, chunks, local, 2, rows, width), bf16),
            vmem((owners, both, width), bf16),
            vmem((4, half // 2, both, width), bf16),
            vmem((2, xs, 2, local, hidden, 128), bf16),
            vmem((xs, 2, local, hidden, 128), bf16),
            vmem((xs - 1, 2, local, hidden, 128), bf16),
            dma((2,)),
            dma((2, half + 1, 2)),
            dma((2, half + 1, 2)),
            dma((heads - 1, chunks)),
            dma((heads - 1, chunks)),
            dma((heads - 1, chunks, local)),
            dma((heads - 1, chunks, local)),
            dma((4, half // 2, 2)),
            dma((4, half // 2, 2)),
            dma((1,)),
            dma((1,)),
            dma((xs - 1,)),
            dma((xs - 1,)),
            dma((heads - 1,)),
            dma((heads - 1,)),
        ],
        compiler_params=pltpu.CompilerParams(
            collective_id=0, has_side_effects=True, vmem_limit_bytes=52 * 1024 * 1024
        ),
        name="experts",
    )(block, weight_in, weight_out)
    return tokens_out[:tokens], tokens_out[tokens:], grads_out[0], grads_out[1]


def solution(mesh):
    in_specs = (
        P(("dp", "expert"), None),
        P(("dp", "expert"), None),
        P(("dp", "expert"), None),
        P(("dp", "expert"), None),
        P("expert", "head", None),
        P("expert", "head", None),
    )
    out_specs = (
        P(("dp", "expert"), None),
        P(("dp", "expert"), None),
        P("expert", "head", "dp"),
        P("expert", "head", "dp"),
    )
    return jax.shard_map(
        on_device, mesh=mesh, in_specs=in_specs, out_specs=out_specs, check_vma=False
    )
```
